32 devices in a mesh: box: 16 (over z, y, core), angle: 2 (over x).
Axes of the slice: x: 2, y: 2, z: 4, core: 2. Of those that a mesh axis runs over, the one named last changes fastest.
Arguments:
- child_field: bfloat16 [1024, 2, 64, 128], P('box', None, 'angle'), may hold values from -6 to 6
- child_list: int32 [1024, 8], P('box'), may hold values from -1 to 1023, as said below
- child_op: int32 [1024, 8], P('box'), may hold values from 0 to 39
- child_home: int32 [1024], replicated, may hold values from 0 to 1023, as said below
- child_ops: bfloat16 [40, 2, 64, 128], P(None, None, 'angle'), may hold values from -2 to 2
- parent_list: int32 [256, 8], P('box'), may hold values from -1 to 255, as said below
- parent_op: int32 [256, 8], P('box'), may hold values from 0 to 39
- parent_home: int32 [256], replicated, may hold values from 0 to 255, as said below
- parent_ops: bfloat16 [40, 2, 128, 256], P(None, None, 'angle'), may hold values from -2 to 2
Outputs:
- child_out: bfloat16 [1024, 2, 64, 128], P('box', None, 'angle')
The draws below stay inside these ranges and needn't reach their ends.
Inputs may be any that keep to these rules, and one draw needn't show every extreme that they name: `child_list`: entries are child box ids, or -1 for an empty slot. Among the list rows held by one index of box, at most 32 entries name boxes whose row child_home lies on one index of box (row // 64); some pair of indices reaches 32 in every draw. Entries may repeat. A permutation: child box i is held in row child_home[i]. `parent_list`: entries are parent box ids, or -1 for an empty slot. Among the list rows held by one index of box, at most 8 entries name boxes whose row parent_home lies on one index of box (row // 16); some pair of indices reaches 8 in every draw. Entries may repeat. A permutation: parent box i is held in row parent_home[i].
All inputs are finite; a program needn't handle non-finite values.
Results may differ from the reference program's by a relative error of at most 0.0017.
The reference program's roundings to bfloat16 on the way (of `stretched`, `parent_field`, `parent_far`, `turned`, `narrowed` and `child_term`) count: a program that leaves them out, or rounds other values in their place, can miss the bound.
Values may be sent and summed in bfloat16 or wider, within the bound.
A program may use at most 128 MiB of HBM per device.

```python
import math
import jax
import jax.numpy as jnp
from jax import lax

CT = 64
SUBBOX_HEADINGS = 128
PT = 128
PP = 256
KIDS = 4
NOPS1 = 40
NOPS2 = 40
L1 = 8
L2 = 8
CB = 64
PB = 16
CHILDREN = 1024
PARENTS = 256


def home_table(key, salt_value, total_rows):
    return jax.random.permutation(jax.random.fold_in(key, salt_value), total_rows).astype(jnp.int32)


def build_lists(key, salt_value, total_rows, rows_device, list_slots):
    home_rows = home_table(key, salt_value, total_rows)
    owners = total_rows // rows_device
    per_device = rows_device * list_slots
    capacity = per_device // owners
    inverse = jnp.argsort(home_rows).astype(jnp.int32)
    base_key = jax.random.fold_in(key, salt_value + 100)
    level_key, count_key, chosen_key, shuffle_key, corner_key = jax.random.split(base_key, 5)
    loading = jax.random.randint(level_key, (owners, 1), 3, 5)
    ceiling = loading * capacity // 4
    counts = jax.random.randint(count_key, (owners, owners), ceiling // 2, ceiling + 1)
    corner = jax.random.randint(corner_key, (2,), 0, owners)
    rows_grid = lax.broadcasted_iota(jnp.int32, (owners, owners), 0)
    cols_grid = lax.broadcasted_iota(jnp.int32, (owners, owners), 1)
    counts = jnp.where((rows_grid == corner[0]) & (cols_grid == corner[1]), capacity, counts)
    slot_index = jnp.arange(per_device, dtype=jnp.int32)
    owner_of = slot_index // capacity
    filled = (slot_index % capacity)[None, :] < counts[:, owner_of]
    chosen = jax.random.randint(chosen_key, (owners, per_device), 0, rows_device)
    box_ids = inverse[owner_of[None, :] * rows_device + chosen]
    entries = jnp.where(filled, box_ids, -1)
    scores = jax.random.randint(shuffle_key, (owners, per_device), 0, 1 << 16) * per_device + slot_index[None, :]
    shuffle = jnp.argsort(scores, axis=1)
    entries = jnp.take_along_axis(entries, shuffle, axis=1)
    return entries.reshape(owners * rows_device, list_slots).astype(jnp.int32)


def draw_child_field(key, part):
    field_key = jax.random.fold_in(key, 7)
    noise_key, amp_key, wave_key, phase_key = jax.random.split(field_key, 4)
    full_shape = (CHILDREN, 2, CT, SUBBOX_HEADINGS)
    stochastic_jitter = jnp.clip(jax.random.normal(noise_key, full_shape, jnp.float32), -3.5, 3.5)
    radiated_magnitude = jax.random.uniform(amp_key, (CHILDREN, 2, 1, 1), jnp.float32, -2.4, 2.4)
    oscillation_multiplier = jax.random.randint(wave_key, (CHILDREN, 2, 1, 1), 0, 4).astype(jnp.float32)
    cyclic_offset = jax.random.uniform(phase_key, (CHILDREN, 2, 1, 1), jnp.float32, -math.pi, math.pi)
    polar = (jnp.arange(CT, dtype=jnp.float32) + 0.5) * (math.pi / CT)
    bounding_profile = (jnp.sin(polar) ** 4)[None, None, :, None]
    heading_radians = jnp.arange(SUBBOX_HEADINGS, dtype=jnp.float32)[None, None, None, :]
    toggling_parity = (1 - 2 * (jnp.arange(SUBBOX_HEADINGS, dtype=jnp.int32) % 2)).astype(jnp.float32)[None, None, None, :]
    oscillating_tone = toggling_parity * jnp.cos(2.0 * math.pi / SUBBOX_HEADINGS * oscillation_multiplier * heading_radians + cyclic_offset)
    return (stochastic_jitter + radiated_magnitude * bounding_profile * oscillating_tone).astype(jnp.bfloat16)


def draw_child_home(key, part):
    return home_table(key, 1, CHILDREN)


def draw_child_list(key, part):
    return build_lists(key, 1, CHILDREN, CB, L1)


def draw_parent_home(key, part):
    return home_table(key, 2, PARENTS)


def draw_parent_list(key, part):
    return build_lists(key, 2, PARENTS, PB, L2)


def plant(array, rng, least, largest):
    longest = array.shape.index(max(array.shape))
    spots = []
    for shift in (0, 1):
        where = [jax.random.randint(jax.random.fold_in(rng, axis), (), 0, length) for axis, length in enumerate(array.shape)]
        where[longest] = (where[longest] + shift) % array.shape[longest]
        spots.append(tuple(where))
    return array.at[spots[0]].set(least).at[spots[1]].set(largest)


def levels(stream_key, dims, shards, smallest, high):
    def one(dim, shards_of):
        draws = jax.random.uniform(jax.random.fold_in(jax.random.fold_in(stream_key, 6), dim), (shards_of,), jnp.float32, smallest / len(shards), high / len(shards))
        return jnp.repeat(jnp.exp(draws), dims[dim] // shards_of).reshape((-1,) + (1,) * (len(dims) - dim - 1))

    factor_of = one(*shards[0])
    for cut in shards[1:]:
        factor_of = factor_of * one(*cut)
    return factor_of


def normal_values(rng, shape, spread, reach, cuts=(), held_as=jnp.bfloat16):
    values = spread * jax.random.normal(rng, shape, jnp.float32)
    if cuts:
        values = values * levels(rng, shape, cuts, -0.22, 0.18)
    return jnp.clip(values, -reach, reach).astype(held_as)


def setup_inputs(seed: int = 0) -> dict:
    seeds = jax.random.split(jax.random.key(seed), 10)
    return {
        "child_field": draw_child_field(jax.random.fold_in(seeds[9], 71), 0),
        "child_list": draw_child_list(jax.random.fold_in(seeds[9], 71), 0),
        "child_op": plant(jax.random.randint(seeds[2], (CHILDREN, L1), 0, NOPS1), jax.random.fold_in(seeds[2], 1), 0, NOPS1 - 1).astype(jnp.int32),
        "child_home": draw_child_home(jax.random.fold_in(seeds[9], 71), 0),
        "child_ops": normal_values(seeds[4], (NOPS1, 2, CT, SUBBOX_HEADINGS), L1 ** -0.5, 2.0, ((2, 2),)),
        "parent_list": draw_parent_list(jax.random.fold_in(seeds[9], 71), 0),
        "parent_op": plant(jax.random.randint(seeds[6], (PARENTS, L2), 0, NOPS2), jax.random.fold_in(seeds[6], 1), 0, NOPS2 - 1).astype(jnp.int32),
        "parent_home": draw_parent_home(jax.random.fold_in(seeds[9], 71), 0),
        "parent_ops": normal_values(seeds[8], (NOPS2, 2, PT, PP), L2 ** -0.5, 2.0, ((2, 2),)),
    }


WAVE_NUMBER = 6.0


def fourier_table(fine_count, coarse_count, offset):
    fine_pos = (jnp.arange(fine_count, dtype=jnp.float32) + offset) / fine_count
    coarse_pos = (jnp.arange(coarse_count, dtype=jnp.float32) + offset) / coarse_count
    distance = fine_pos[:, None] - coarse_pos[None, :]
    harmonic = jnp.arange(1, coarse_count // 2, dtype=jnp.float32)
    cosines = jnp.cos((2.0 * math.pi) * harmonic[None, None, :] * distance[:, :, None])
    summed = 1.0 + 2.0 * jnp.sum(cosines, axis=2) + jnp.cos(math.pi * coarse_count * distance)
    return summed / coarse_count


def shift_parts(polar_rows):
    polar_angle = math.pi * (polar_rows.astype(jnp.float32) + 0.5) / PT
    heading_radians = (2.0 * math.pi / PP) * jnp.arange(PP, dtype=jnp.float32)
    kid_index = jnp.arange(KIDS, dtype=jnp.int32)
    side_x = (2 * (kid_index % 2) - 1).astype(jnp.float32)
    side_y = (2 * ((kid_index // 2) % 2) - 1).astype(jnp.float32)
    across = side_x[:, None] * jnp.cos(heading_radians)[None, :] + side_y[:, None] * jnp.sin(heading_radians)[None, :]
    phase_arg = WAVE_NUMBER * jnp.sin(polar_angle)[None, :, None] * across[:, None, :]
    return jnp.cos(phase_arg), jnp.sin(phase_arg)


def lift_sum(widened, cos_part, sin_part):
    real_part = jnp.sum(cos_part * widened[..., 0, :, :] - sin_part * widened[..., 1, :, :], axis=-3)
    imag_part = jnp.sum(cos_part * widened[..., 1, :, :] + sin_part * widened[..., 0, :, :], axis=-3)
    return jnp.stack([real_part, imag_part], axis=-3).astype(jnp.bfloat16)


def lower_turn(parents, cos_part, sin_part):
    real_in = jnp.expand_dims(parents[..., 0, :, :].astype(jnp.float32), -3)
    imag_in = jnp.expand_dims(parents[..., 1, :, :].astype(jnp.float32), -3)
    real_out = cos_part * real_in + sin_part * imag_in
    imag_out = cos_part * imag_in - sin_part * real_in
    return jnp.stack([real_out, imag_out], axis=-3).astype(jnp.bfloat16)


def far_sum(patterns, far_lists, op_index, home_rows, op_table, block_rows):
    blocks = far_lists.shape[0] // block_rows
    slot_count = far_lists.shape[1]

    def per_block(block_pair):
        box_ids, op_rows = block_pair
        usable = box_ids >= 0
        source = patterns[home_rows[jnp.where(usable, box_ids, 0)]].astype(jnp.float32)
        translator = op_table[op_rows].astype(jnp.float32)
        weight = usable.astype(jnp.float32)[:, :, None, None]
        real_part = jnp.sum(weight * (translator[:, :, 0] * source[:, :, 0] - translator[:, :, 1] * source[:, :, 1]), axis=1)
        imag_part = jnp.sum(weight * (translator[:, :, 0] * source[:, :, 1] + translator[:, :, 1] * source[:, :, 0]), axis=1)
        return jnp.stack([real_part, imag_part], axis=1)

    summed = lax.map(per_block, (far_lists.reshape(blocks, block_rows, slot_count), op_index.reshape(blocks, block_rows, slot_count)))
    return summed.reshape((far_lists.shape[0],) + patterns.shape[1:])


def reference(child_field, child_list, child_op, child_home, child_ops, parent_list, parent_op, parent_home, parent_ops):
    child_far = far_sum(child_field, child_list, child_op, child_home, child_ops, CB)
    theta_up = fourier_table(PT, CT, 0.5).astype(jnp.bfloat16)
    phi_up = fourier_table(PP, SUBBOX_HEADINGS, 0.0).T.astype(jnp.bfloat16)
    theta_down = (fourier_table(PT, CT, 0.5).T * (CT / PT)).astype(jnp.bfloat16)
    phi_down = (fourier_table(PP, SUBBOX_HEADINGS, 0.0) * (SUBBOX_HEADINGS / PP)).astype(jnp.bfloat16)
    cos_part, sin_part = shift_parts(jnp.arange(PT, dtype=jnp.int32))
    blocks = PARENTS // PB
    grouped = child_field.reshape(blocks, PB, KIDS, 2, CT, SUBBOX_HEADINGS)

    def lift_block(kid_block):
        stretched = jnp.einsum("ut,qkctp->qkcup", theta_up.astype(jnp.float32), kid_block.astype(jnp.float32), precision=lax.Precision.HIGHEST).astype(jnp.bfloat16)
        widened = jnp.einsum("qkcup,pv->qkcuv", stretched.astype(jnp.float32), phi_up.astype(jnp.float32), precision=lax.Precision.HIGHEST)
        return lift_sum(widened, cos_part, sin_part)

    parent_field = lax.map(lift_block, grouped).reshape(PARENTS, 2, PT, PP)
    parent_far = far_sum(parent_field, parent_list, parent_op, parent_home, parent_ops, PB).astype(jnp.bfloat16)

    def lower_block(parents):
        turned = lower_turn(parents, cos_part, sin_part)
        narrowed = jnp.einsum("qkcuv,vp->qkcup", turned.astype(jnp.float32), phi_down.astype(jnp.float32), precision=lax.Precision.HIGHEST).astype(jnp.bfloat16)
        terms = jnp.einsum("tu,qkcup->qkctp", theta_down.astype(jnp.float32), narrowed.astype(jnp.float32), precision=lax.Precision.HIGHEST)
        return terms.astype(jnp.bfloat16)

    child_term = lax.map(lower_block, parent_far.reshape(blocks, PB, 2, PT, PP)).reshape(CHILDREN, 2, CT, SUBBOX_HEADINGS)
    child_term = lax.optimization_barrier(child_term)
    return (child_far + child_term.astype(jnp.float32)).astype(jnp.bfloat16)
```

```python
import functools
import math

import jax
import jax.numpy as jnp
from jax import lax
from jax.experimental import pallas as pl
from jax.experimental.pallas import tpu as pltpu
from jax.sharding import PartitionSpec as P

CT = 64
SUBBOX_HEADINGS = 128
PT = 128
PP = 256
KIDS = 4
WAVE_NUMBER = 6.0


def waves(count, offset, half):
    doubled = (2 * jnp.arange(count, dtype=jnp.int32) + int(2 * offset))[:, None]
    harmonic = jnp.arange(half + 1, dtype=jnp.int32)[None, :]
    turns = (doubled * harmonic) % (2 * count)
    angle = turns.astype(jnp.float32) * (math.pi / count)
    return jnp.cos(angle), jnp.sin(angle)


def fourier_table(fine_count, coarse_count, offset):
    half = coarse_count // 2
    fine_cos, fine_sin = waves(fine_count, offset, half)
    coarse_cos, coarse_sin = waves(coarse_count, offset, half)
    order = jnp.arange(half + 1)
    weight = jnp.where((order == 0) | (order == half), 1.0, 2.0) / coarse_count
    fine = jnp.concatenate([fine_cos * weight, fine_sin * weight], axis=1)
    coarse = jnp.concatenate([coarse_cos, coarse_sin], axis=1)
    return jnp.dot(fine, coarse.T, precision=lax.Precision.HIGHEST)


def shift_parts(polar_rows):
    polar_angle = math.pi * (polar_rows.astype(jnp.float32) + 0.5) / PT
    heading_radians = 2.0 * math.pi / PP * jnp.arange(PP, dtype=jnp.float32)
    kid_index = jnp.arange(KIDS, dtype=jnp.int32)
    side_x = (2 * (kid_index % 2) - 1).astype(jnp.float32)
    side_y = (2 * (kid_index // 2 % 2) - 1).astype(jnp.float32)
    across = (
        side_x[:, None] * jnp.cos(heading_radians)[None, :]
        + side_y[:, None] * jnp.sin(heading_radians)[None, :]
    )
    phase_arg = WAVE_NUMBER * jnp.sin(polar_angle)[None, :, None] * across[:, None, :]
    return (jnp.cos(phase_arg), jnp.sin(phase_arg))


def lift_sum(widened, cos_part, sin_part):
    real_part = jnp.sum(
        cos_part * widened[..., 0, :, :] - sin_part * widened[..., 1, :, :], axis=-3
    )
    imag_part = jnp.sum(
        cos_part * widened[..., 1, :, :] + sin_part * widened[..., 0, :, :], axis=-3
    )
    return jnp.stack([real_part, imag_part], axis=-3).astype(jnp.bfloat16)


def lower_turn(parents, cos_part, sin_part):
    real_in = jnp.expand_dims(parents[..., 0, :, :].astype(jnp.float32), -3)
    imag_in = jnp.expand_dims(parents[..., 1, :, :].astype(jnp.float32), -3)
    real_out = cos_part * real_in + sin_part * imag_in
    imag_out = cos_part * imag_in - sin_part * real_in
    return jnp.stack([real_out, imag_out], axis=-3).astype(jnp.bfloat16)


def far_kernel(span, list_ref, op_ref, home_ref, field_ref, ops_ref, out_ref, padded):
    rows, slots = list_ref.shape
    empty = ops_ref.shape[0]
    padded[0:empty] = ops_ref[...]
    padded[empty] = jnp.zeros_like(padded[empty])
    thin = out_ref.shape[2]

    def row(r, carry):
        homes, opers = [], []
        for j in range(slots):
            box = list_ref[r, j]
            homes.append(home_ref[jnp.maximum(box, 0)])
            opers.append(jnp.where(box >= 0, op_ref[r, j], empty))
        for start in range(0, thin, span):
            part = pl.ds(start, span)
            real = imag = None
            for j in range(slots):
                a = padded[opers[j], 0, part, :].astype(jnp.float32)
                b = padded[opers[j], 1, part, :].astype(jnp.float32)
                c = field_ref[homes[j], 0, part, :].astype(jnp.float32)
                d = field_ref[homes[j], 1, part, :].astype(jnp.float32)
                re, im = a * c - b * d, a * d + b * c
                real = re if real is None else real + re
                imag = im if imag is None else imag + im
            out_ref[r, 0, part, :] = real.astype(out_ref.dtype)
            out_ref[r, 1, part, :] = imag.astype(out_ref.dtype)
        return carry

    lax.fori_loop(0, rows, row, 0)


def far_sum(field, lists, ops, homes, table, dtype):
    rows, slots = lists.shape
    shape = field.shape[1:]
    span = min(shape[1], 4096 // shape[2])
    smem = pl.BlockSpec(memory_space=pltpu.SMEM)
    vmem = pl.BlockSpec(memory_space=pltpu.VMEM)
    return pl.pallas_call(
        functools.partial(far_kernel, span),
        out_shape=jax.ShapeDtypeStruct((rows,) + shape, dtype),
        in_specs=[smem, smem, smem, vmem, vmem],
        out_specs=vmem,
        scratch_shapes=[pltpu.VMEM((table.shape[0] + 1,) + table.shape[1:], table.dtype)],
        compiler_params=pltpu.CompilerParams(vmem_limit_bytes=32 * 2**20),
        cost_estimate=pl.CostEstimate(
            flops=rows * slots * math.prod(shape) * 4,
            bytes_accessed=field.size * 2 + table.size * 2,
            transcendentals=0,
        ),
    )(lists, ops, homes, field, table)


def local(
    child_field,
    child_list,
    child_op,
    child_home,
    child_ops,
    parent_list,
    parent_op,
    parent_home,
    parent_ops,
):
    angle_index = lax.axis_index("angle")
    child_rows = child_field.shape[0]
    parent_rows = parent_list.shape[0]
    child_thin = child_field.shape[2]
    parent_thin = parent_ops.shape[2]
    whole_polar = lax.all_gather(child_field, "angle", axis=2, tiled=True)
    child_all = lax.all_gather(child_field, "box", axis=0, tiled=True)
    theta = fourier_table(PT, CT, 0.5)
    phi = fourier_table(PP, SUBBOX_HEADINGS, 0.0)
    theta_up = theta.astype(jnp.bfloat16)
    phi_up = phi.T.astype(jnp.bfloat16)
    theta_down = (theta.T * (CT / PT)).astype(jnp.bfloat16)
    phi_down = (phi * (SUBBOX_HEADINGS / PP)).astype(jnp.bfloat16)
    up_rows = lax.dynamic_slice_in_dim(theta_up, angle_index * parent_thin, parent_thin, 0)
    stretched = jnp.einsum(
        "ut,rctp->rcup", up_rows, whole_polar, preferred_element_type=jnp.float32
    ).astype(jnp.bfloat16)
    widened = jnp.einsum("rcup,pv->rcuv", stretched, phi_up, preferred_element_type=jnp.float32)
    local_polar = angle_index * parent_thin + jnp.arange(parent_thin, dtype=jnp.int32)
    cos_local, sin_local = shift_parts(local_polar)
    parent_field = lift_sum(
        widened.reshape(parent_rows, KIDS, 2, parent_thin, PP), cos_local, sin_local
    )
    parent_all = lax.all_gather(parent_field, "box", axis=0, tiled=True)
    child_far = far_sum(child_all, child_list, child_op, child_home, child_ops, jnp.float32)
    parent_far = far_sum(
        parent_all, parent_list, parent_op, parent_home, parent_ops, jnp.bfloat16
    )
    down_rows = lax.dynamic_slice_in_dim(theta_down, angle_index * child_thin, child_thin, 0)
    parents = lax.all_gather(parent_far, "angle", axis=2, tiled=True)
    cos_piece, sin_piece = shift_parts(jnp.arange(PT, dtype=jnp.int32))
    turned = lower_turn(parents, cos_piece, sin_piece)
    narrowed = jnp.einsum(
        "qkcuv,vp->qkcup", turned, phi_down, preferred_element_type=jnp.float32
    ).astype(jnp.bfloat16)
    summed_term = jnp.einsum(
        "tu,qkcup->qkctp", down_rows, narrowed, preferred_element_type=jnp.float32
    )
    child_term = summed_term.astype(jnp.bfloat16).reshape(
        child_rows, 2, child_thin, SUBBOX_HEADINGS
    )
    child_term = lax.optimization_barrier(child_term)
    return (child_far + child_term.astype(jnp.float32)).astype(jnp.bfloat16)


def solution(mesh):
    return jax.shard_map(
        local,
        mesh=mesh,
        in_specs=(
            P("box", None, "angle", None),
            P("box", None),
            P("box", None),
            P(),
            P(None, None, "angle", None),
            P("box", None),
            P("box", None),
            P(),
            P(None, None, "angle", None),
        ),
        out_specs=P("box", None, "angle", None),
        check_vma=False,
    )
```

```python
import functools
import math

import jax
import jax.numpy as jnp
from jax import lax
from jax.experimental import pallas as pl
from jax.experimental.pallas import tpu as pltpu
from jax.sharding import PartitionSpec as P

CT = 64
SUBBOX_HEADINGS = 128
PT = 128
PP = 256
KIDS = 4
WAVE_NUMBER = 6.0


def waves(count, offset, half):
    doubled = (2 * jnp.arange(count, dtype=jnp.int32) + int(2 * offset))[:, None]
    harmonic = jnp.arange(half + 1, dtype=jnp.int32)[None, :]
    turns = (doubled * harmonic) % (2 * count)
    angle = turns.astype(jnp.float32) * (math.pi / count)
    return jnp.cos(angle), jnp.sin(angle)


def fourier_table(fine_count, coarse_count, offset):
    half = coarse_count // 2
    fine_cos, fine_sin = waves(fine_count, offset, half)
    coarse_cos, coarse_sin = waves(coarse_count, offset, half)
    order = jnp.arange(half + 1)
    weight = jnp.where((order == 0) | (order == half), 1.0, 2.0) / coarse_count
    fine = jnp.concatenate([fine_cos * weight, fine_sin * weight], axis=1)
    coarse = jnp.concatenate([coarse_cos, coarse_sin], axis=1)
    return jnp.dot(fine, coarse.T, precision=lax.Precision.HIGHEST)


def shift_parts(polar_rows):
    polar_angle = math.pi * (polar_rows.astype(jnp.float32) + 0.5) / PT
    heading_radians = 2.0 * math.pi / PP * jnp.arange(PP, dtype=jnp.float32)
    kid_index = jnp.arange(KIDS, dtype=jnp.int32)
    side_x = (2 * (kid_index % 2) - 1).astype(jnp.float32)
    side_y = (2 * (kid_index // 2 % 2) - 1).astype(jnp.float32)
    across = (
        side_x[:, None] * jnp.cos(heading_radians)[None, :]
        + side_y[:, None] * jnp.sin(heading_radians)[None, :]
    )
    phase_arg = WAVE_NUMBER * jnp.sin(polar_angle)[None, :, None] * across[:, None, :]
    return (jnp.cos(phase_arg), jnp.sin(phase_arg))


def lift_sum(widened, cos_part, sin_part):
    real_part = jnp.sum(
        cos_part * widened[..., 0, :, :] - sin_part * widened[..., 1, :, :], axis=-3
    )
    imag_part = jnp.sum(
        cos_part * widened[..., 1, :, :] + sin_part * widened[..., 0, :, :], axis=-3
    )
    return jnp.stack([real_part, imag_part], axis=-3).astype(jnp.bfloat16)


def lower_turn(parents, cos_part, sin_part):
    real_in = jnp.expand_dims(parents[..., 0, :, :].astype(jnp.float32), -3)
    imag_in = jnp.expand_dims(parents[..., 1, :, :].astype(jnp.float32), -3)
    real_out = cos_part * real_in + sin_part * imag_in
    imag_out = cos_part * imag_in - sin_part * real_in
    return jnp.stack([real_out, imag_out], axis=-3).astype(jnp.bfloat16)


def far_kernel(span, list_ref, op_ref, home_ref, field_ref, ops_ref, out_ref, padded):
    rows, slots = list_ref.shape
    empty = ops_ref.shape[0]
    padded[0:empty] = ops_ref[...]
    padded[empty] = jnp.zeros_like(padded[empty])
    thin = out_ref.shape[2]

    def row(r, carry):
        homes, opers = [], []
        for j in range(slots):
            box = list_ref[r, j]
            homes.append(home_ref[jnp.maximum(box, 0)])
            opers.append(jnp.where(box >= 0, op_ref[r, j], empty))
        for start in range(0, thin, span):
            part = pl.ds(start, span)
            real = imag = None
            for j in range(slots):
                a = padded[opers[j], 0, part, :].astype(jnp.float32)
                b = padded[opers[j], 1, part, :].astype(jnp.float32)
                c = field_ref[homes[j], 0, part, :].astype(jnp.float32)
                d = field_ref[homes[j], 1, part, :].astype(jnp.float32)
                re, im = a * c - b * d, a * d + b * c
                real = re if real is None else real + re
                imag = im if imag is None else imag + im
            out_ref[r, 0, part, :] = real.astype(out_ref.dtype)
            out_ref[r, 1, part, :] = imag.astype(out_ref.dtype)
        return carry

    lax.fori_loop(0, rows, row, 0)


def far_sum(field, lists, ops, homes, table, dtype):
    rows, slots = lists.shape
    shape = field.shape[1:]
    span = min(shape[1], 4096 // shape[2])
    smem = pl.BlockSpec(memory_space=pltpu.SMEM)
    vmem = pl.BlockSpec(memory_space=pltpu.VMEM)
    return pl.pallas_call(
        functools.partial(far_kernel, span),
        out_shape=jax.ShapeDtypeStruct((rows,) + shape, dtype),
        in_specs=[smem, smem, smem, vmem, vmem],
        out_specs=vmem,
        scratch_shapes=[pltpu.VMEM((table.shape[0] + 1,) + table.shape[1:], table.dtype)],
        compiler_params=pltpu.CompilerParams(vmem_limit_bytes=32 * 2**20),
        cost_estimate=pl.CostEstimate(
            flops=rows * slots * math.prod(shape) * 4,
            bytes_accessed=field.size * 2 + table.size * 2,
            transcendentals=0,
        ),
    )(lists, ops, homes, field, table)


Z, Y, C = 4, 2, 2
UP, DOWN, SIDE, CORE, PAIR = range(5)
CHUNKS = 4


class Gather:
    def __init__(self, own, slots, rows, send, recv, place):
        self.own, self.slots, self.rows, self.send, self.recv = own, slots, rows, send, recv
        self.z, self.y, self.c = place
        self.started = []

    def slot(self, z, y, c):
        return (z * Y + y) * C + c

    def part(self, slot, h):
        half = self.rows // 2
        return self.slots.at[pl.ds(slot * self.rows + h * half, half)]

    def copy(self, slot, h, way, target, first=False):
        half = self.rows // 2
        source = self.own.at[pl.ds(h * half, half)] if first else self.part(slot, h)
        return pltpu.make_async_remote_copy(
            src_ref=source,
            dst_ref=self.part(slot, h),
            send_sem=self.send.at[way, slot, h],
            recv_sem=self.recv.at[slot, h],
            device_id={"box": target},
            device_id_type=pl.DeviceIdType.MESH,
        )

    def go(self, cond, *args, **kw):
        copy = self.copy(*args, **kw)
        self.started.append((cond, copy))
        pl.when(cond)(lambda: copy.start()) if cond is not None else copy.start()

    def near(self, way):
        z, y, c = self.z, self.y, self.c
        if way == UP:
            return self.slot(jnp.minimum(z + 1, Z - 1), y, c)
        if way == DOWN:
            return self.slot(jnp.maximum(z - 1, 0), y, c)
        if way == SIDE:
            return self.slot(z, 1 - y, c)
        if way == CORE:
            return self.slot(z, y, 1 - c)
        return self.slot(z + 1 - 2 * (z % 2), y, c)

    def arrived(self, cond, slot, h):
        copy = self.copy(slot, h, CORE, self.near(CORE))
        pl.when(cond)(lambda: copy.wait_recv()) if cond is not None else copy.wait_recv()

    def first(self, h):
        mine = self.slot(self.z, self.y, self.c)
        self.go(self.z < Z - 1, mine, h, UP, self.near(UP), first=True)
        self.go(self.z > 0, mine, h, DOWN, self.near(DOWN), first=True)
        self.go(None, mine, h, SIDE, self.near(SIDE), first=True)
        self.go(None, mine, h, CORE, self.near(CORE), first=True)

    def across(self, d):
        for sign in (-1, 1) if d else (1,):
            there = self.z + sign * d
            valid = None if d == 0 else (there >= 0) & (there < Z)
            slot = self.slot(jnp.clip(there, 0, Z - 1), 1 - self.y, self.c)
            for h in range(2):
                self.arrived(valid, slot, h)
                self.go(valid, slot, h, CORE, self.near(CORE))
                if d == 0 and h == 1:
                    self.go(None, slot, h, PAIR, self.near(PAIR))

    def step(self, d):
        for h in range(2):
            for sign in (-1, 1):
                there = self.z + sign * d
                valid = (there >= 0) & (there < Z)
                slot = self.slot(jnp.clip(there, 0, Z - 1), self.y, self.c)
                self.arrived(valid, slot, h)
                onward = valid & ((self.z < Z - 1) if sign < 0 else (self.z > 0))
                self.go(onward, slot, h, UP if sign < 0 else DOWN, self.near(UP if sign < 0 else DOWN))
                side = valid
                if d == 1 and h == 1:
                    side = valid & ((self.z % 2 == 1) if sign < 0 else (self.z % 2 == 0))
                    side = valid & jnp.logical_not(side)
                self.go(side, slot, h, SIDE, self.near(SIDE))
                self.go(valid, slot, h, CORE, self.near(CORE))
        self.across(d - 1)

    def finish(self):
        self.across(Z - 1)
        for z in range(Z):
            for y in range(Y):
                for h in range(2):
                    self.arrived(None, self.slot(z, y, 1 - self.c), h)

    def drain(self):
        for cond, copy in self.started:
            pl.when(cond)(lambda copy=copy: copy.wait_send()) if cond is not None else copy.wait_send()


def translate(lists, op, home, field, padded, r, empty, start, span):
    part = pl.ds(start, span)
    real = imag = None
    for j in range(lists.shape[1]):
        box = lists[r, j]
        at = home[jnp.maximum(box, 0)]
        oper = jnp.where(box >= 0, op[r, j], empty)
        a = padded[oper, 0, part, :].astype(jnp.float32)
        b = padded[oper, 1, part, :].astype(jnp.float32)
        c = field[at, 0, part, :].astype(jnp.float32)
        d = field[at, 1, part, :].astype(jnp.float32)
        re, im = a * c - b * d, a * d + b * c
        real = re if real is None else real + re
        imag = im if imag is None else imag + im
    return real, imag


def whole_kernel(
    child_field, child_list, child_op, child_home, child_ops,
    parent_list, parent_op, parent_home, parent_ops,
    theta_up, phi_up, theta_down, phi_down, cos_ref, sin_ref,
    out_ref,
    child_all, parent_all, polar, child_pad, parent_pad, far, terms,
    c_send, c_recv, p_send, p_recv, x_send, x_recv, f_send, f_recv, here,
):
    box, angle = lax.axis_index("box"), lax.axis_index("angle")
    z, y, c = box // (Y * C), (box // C) % Y, box % C
    children, child_thin = child_field.shape[0], child_field.shape[2]
    parents, parent_thin = parent_list.shape[0], far.shape[3]
    kids_rows, group = children // CHUNKS, parents // CHUNKS
    child_empty, parent_empty = child_ops.shape[0], parent_ops.shape[0]
    MESH = pl.DeviceIdType.MESH
    children_of = Gather(child_field, child_all, children, c_send, c_recv, (z, y, c))
    mine = parent_all.at[pl.ds(box * parents, parents)]
    parents_of = Gather(mine, parent_all, parents, p_send, p_recv, (z, y, c))
    other = {"angle": 1 - angle}

    locals_ = [
        pltpu.make_async_copy(child_field, polar.at[angle], here.at[0]),
        pltpu.make_async_copy(child_field, child_all.at[pl.ds(box * children, children)], here.at[1]),
        pltpu.make_async_copy(child_ops, child_pad.at[pl.ds(0, child_empty)], here.at[2]),
        pltpu.make_async_copy(parent_ops, parent_pad.at[pl.ds(0, parent_empty)], here.at[3]),
    ]
    for copy in locals_:
        copy.start()

    barrier = pltpu.get_barrier_semaphore()
    for way in (SIDE, CORE):
        pl.semaphore_signal(barrier, inc=1, device_id={"box": children_of.near(way)}, device_id_type=MESH)
    pl.semaphore_signal(barrier, inc=1, device_id=other, device_id_type=MESH)

    @pl.when(z < Z - 1)
    def _():
        pl.semaphore_signal(barrier, inc=1, device_id={"box": children_of.near(UP)}, device_id_type=MESH)

    @pl.when(z > 0)
    def _():
        pl.semaphore_signal(barrier, inc=1, device_id={"box": children_of.near(DOWN)}, device_id_type=MESH)

    pl.semaphore_wait(barrier, 5 - (z == 0).astype(jnp.int32) - (z == Z - 1).astype(jnp.int32))

    crossing = []
    for i in range(CHUNKS):
        rows = pl.ds(i * kids_rows, kids_rows)
        crossing.append(
            pltpu.make_async_remote_copy(
                src_ref=child_field.at[rows], dst_ref=polar.at[angle, rows],
                send_sem=x_send.at[i], recv_sem=x_recv.at[i],
                device_id=other, device_id_type=MESH,
            )
        )
        crossing[-1].start()
    for h in range(2):
        children_of.first(h)
    child_pad[child_empty] = jnp.zeros(child_pad.shape[1:], child_pad.dtype)
    parent_pad[parent_empty] = jnp.zeros(parent_pad.shape[1:], parent_pad.dtype)
    for copy in locals_:
        copy.wait()

    up = theta_up[pl.ds(pl.multiple_of(angle * parent_thin, parent_thin), parent_thin), :]
    here_rows = pl.ds(pl.multiple_of(angle * parent_thin, parent_thin), parent_thin)

    def lift(q, carry):
        columns = [
            jnp.concatenate([polar[0, q * KIDS + k, ri], polar[1, q * KIDS + k, ri]], axis=0)
            for k in range(KIDS) for ri in range(2)
        ]
        stretched = jnp.dot(
            up, jnp.concatenate(columns, axis=1), preferred_element_type=jnp.float32
        ).astype(jnp.bfloat16)
        stacked = jnp.concatenate(
            [stretched[:, i * SUBBOX_HEADINGS : (i + 1) * SUBBOX_HEADINGS] for i in range(2 * KIDS)],
            axis=0,
        )
        wide = jnp.dot(stacked, phi_up[...], preferred_element_type=jnp.float32)
        real = imag = 0.0
        for k in range(KIDS):
            co, si = cos_ref[k, here_rows, :], sin_ref[k, here_rows, :]
            wr = wide[2 * k * parent_thin : (2 * k + 1) * parent_thin]
            wi = wide[(2 * k + 1) * parent_thin : (2 * k + 2) * parent_thin]
            real = real + (co * wr - si * wi)
            imag = imag + (co * wi + si * wr)
        parent_all[box * parents + q, 0] = real.astype(jnp.bfloat16)
        parent_all[box * parents + q, 1] = imag.astype(jnp.bfloat16)
        return carry

    for i in range(CHUNKS):
        crossing[i].wait_recv()
        lax.fori_loop(i * group, (i + 1) * group, lift, 0)
        if i % 2:
            parents_of.first(i // 2)

    parents_of.step(1)
    children_of.step(1)
    parents_of.step(2)
    parents_of.step(3)
    parents_of.finish()
    children_of.step(2)

    span = min(parent_thin, 4096 // PP)

    def parent_row(r, carry):
        for start in range(0, parent_thin, span):
            real, imag = translate(
                parent_list, parent_op, parent_home, parent_all, parent_pad, r, parent_empty, start, span
            )
            far[angle, r, 0, pl.ds(start, span), :] = real.astype(jnp.bfloat16)
            far[angle, r, 1, pl.ds(start, span), :] = imag.astype(jnp.bfloat16)
        return carry

    back = []
    for i in range(CHUNKS):
        lax.fori_loop(i * group, (i + 1) * group, parent_row, 0)
        rows = far.at[angle, pl.ds(i * group, group)]
        back.append(
            pltpu.make_async_remote_copy(
                src_ref=rows, dst_ref=rows, send_sem=f_send.at[i], recv_sem=f_recv.at[i],
                device_id=other, device_id_type=MESH,
            )
        )
        back[-1].start()

    down = theta_down[pl.ds(pl.multiple_of(angle * child_thin, child_thin), child_thin), :]

    def lower(q, carry):
        turned = []
        for k in range(KIDS):
            reals, imags = [], []
            for a in range(PT // parent_thin):
                rows = pl.ds(a * parent_thin, parent_thin)
                co, si = cos_ref[k, rows, :], sin_ref[k, rows, :]
                real, imag = far[a, q, 0].astype(jnp.float32), far[a, q, 1].astype(jnp.float32)
                reals.append((co * real + si * imag).astype(jnp.bfloat16))
                imags.append((co * imag - si * real).astype(jnp.bfloat16))
            turned += reals + imags
        narrowed = jnp.dot(
            jnp.concatenate(turned, axis=0), phi_down[...], preferred_element_type=jnp.float32
        ).astype(jnp.bfloat16)
        columns = jnp.concatenate([narrowed[i * PT : (i + 1) * PT] for i in range(2 * KIDS)], axis=1)
        summed = jnp.dot(down, columns, preferred_element_type=jnp.float32).astype(jnp.bfloat16)
        for k in range(KIDS):
            for ri in range(2):
                i = 2 * k + ri
                terms[q * KIDS + k, ri] = summed[:, i * SUBBOX_HEADINGS : (i + 1) * SUBBOX_HEADINGS]
        return carry

    for i in range(CHUNKS):
        back[i].wait_recv()
        lax.fori_loop(i * group, (i + 1) * group, lower, 0)

    children_of.step(3)
    children_of.finish()

    def child_row(r, carry):
        real, imag = translate(
            child_list, child_op, child_home, child_all, child_pad, r, child_empty, 0, child_thin
        )
        out_ref[r, 0] = (real + terms[r, 0].astype(jnp.float32)).astype(jnp.bfloat16)
        out_ref[r, 1] = (imag + terms[r, 1].astype(jnp.float32)).astype(jnp.bfloat16)
        return carry

    lax.fori_loop(0, children, child_row, 0)
    children_of.drain()
    parents_of.drain()
    for copy in crossing + back:
        copy.wait_send()


def whole(fields, tables):
    child_field, child_list, _, _, child_ops, parent_list, _, _, parent_ops = fields
    owners, angles = lax.axis_size("box"), lax.axis_size("angle")
    parent_shape = (parent_list.shape[0], 2) + parent_ops.shape[2:]
    smem = pl.BlockSpec(memory_space=pltpu.SMEM)
    vmem = pl.BlockSpec(memory_space=pltpu.VMEM)
    hbm = pl.BlockSpec(memory_space=pl.ANY)
    bf16 = jnp.bfloat16
    dma = pltpu.SemaphoreType.DMA
    return pl.pallas_call(
        whole_kernel,
        out_shape=jax.ShapeDtypeStruct(child_field.shape, bf16),
        in_specs=[hbm, smem, smem, smem, hbm, smem, smem, smem, hbm] + [vmem] * 6,
        out_specs=vmem,
        scratch_shapes=[
            pltpu.VMEM((owners * child_field.shape[0],) + child_field.shape[1:], bf16),
            pltpu.VMEM((owners * parent_shape[0],) + parent_shape[1:], bf16),
            pltpu.VMEM((angles,) + child_field.shape, bf16),
            pltpu.VMEM((child_ops.shape[0] + 1,) + child_ops.shape[1:], bf16),
            pltpu.VMEM((parent_ops.shape[0] + 1,) + parent_ops.shape[1:], bf16),
            pltpu.VMEM((angles,) + parent_shape, bf16),
            pltpu.VMEM(child_field.shape, bf16),
            dma((5, owners, 2)),
            dma((owners, 2)),
            dma((5, owners, 2)),
            dma((owners, 2)),
            dma((CHUNKS,)),
            dma((CHUNKS,)),
            dma((CHUNKS,)),
            dma((CHUNKS,)),
            dma((4,)),
        ],
        compiler_params=pltpu.CompilerParams(
            collective_id=0, has_side_effects=True, vmem_limit_bytes=58 * 2**20
        ),
    )(*fields, *tables)


def local(
    child_field,
    child_list,
    child_op,
    child_home,
    child_ops,
    parent_list,
    parent_op,
    parent_home,
    parent_ops,
):
    angle_index = lax.axis_index("angle")
    child_rows = child_field.shape[0]
    parent_rows = parent_list.shape[0]
    child_thin = child_field.shape[2]
    parent_thin = parent_ops.shape[2]
    theta = fourier_table(PT, CT, 0.5)
    phi = fourier_table(PP, SUBBOX_HEADINGS, 0.0)
    theta_up = theta.astype(jnp.bfloat16)
    phi_up = phi.T.astype(jnp.bfloat16)
    theta_down = (theta.T * (CT / PT)).astype(jnp.bfloat16)
    phi_down = (phi * (SUBBOX_HEADINGS / PP)).astype(jnp.bfloat16)
    cos_piece, sin_piece = shift_parts(jnp.arange(PT, dtype=jnp.int32))
    if (lax.axis_size("box"), lax.axis_size("angle")) == (Z * Y * C, 2):
        fields = (
            child_field, child_list, child_op, child_home, child_ops,
            parent_list, parent_op, parent_home, parent_ops,
        )
        return whole(fields, (theta_up, phi_up, theta_down, phi_down, cos_piece, sin_piece))
    whole_polar = lax.all_gather(child_field, "angle", axis=2, tiled=True)
    child_all = lax.all_gather(child_field, "box", axis=0, tiled=True)
    up_rows = lax.dynamic_slice_in_dim(theta_up, angle_index * parent_thin, parent_thin, 0)
    stretched = jnp.einsum(
        "ut,rctp->rcup", up_rows, whole_polar, preferred_element_type=jnp.float32
    ).astype(jnp.bfloat16)
    widened = jnp.einsum("rcup,pv->rcuv", stretched, phi_up, preferred_element_type=jnp.float32)
    local_polar = angle_index * parent_thin + jnp.arange(parent_thin, dtype=jnp.int32)
    cos_local, sin_local = shift_parts(local_polar)
    parent_field = lift_sum(
        widened.reshape(parent_rows, KIDS, 2, parent_thin, PP), cos_local, sin_local
    )
    parent_all = lax.all_gather(parent_field, "box", axis=0, tiled=True)
    child_far = far_sum(child_all, child_list, child_op, child_home, child_ops, jnp.float32)
    parent_far = far_sum(
        parent_all, parent_list, parent_op, parent_home, parent_ops, jnp.bfloat16
    )
    down_rows = lax.dynamic_slice_in_dim(theta_down, angle_index * child_thin, child_thin, 0)
    parents = lax.all_gather(parent_far, "angle", axis=2, tiled=True)
    turned = lower_turn(parents, cos_piece, sin_piece)
    narrowed = jnp.einsum(
        "qkcuv,vp->qkcup", turned, phi_down, preferred_element_type=jnp.float32
    ).astype(jnp.bfloat16)
    summed_term = jnp.einsum(
        "tu,qkcup->qkctp", down_rows, narrowed, preferred_element_type=jnp.float32
    )
    child_term = summed_term.astype(jnp.bfloat16).reshape(
        child_rows, 2, child_thin, SUBBOX_HEADINGS
    )
    child_term = lax.optimization_barrier(child_term)
    return (child_far + child_term.astype(jnp.float32)).astype(jnp.bfloat16)


def solution(mesh):
    return jax.shard_map(
        local,
        mesh=mesh,
        in_specs=(
            P("box", None, "angle", None),
            P("box", None),
            P("box", None),
            P(),
            P(None, None, "angle", None),
            P("box", None),
            P("box", None),
            P(),
            P(None, None, "angle", None),
        ),
        out_specs=P("box", None, "angle", None),
        check_vma=False,
    )
```

```python
import functools
import math

import jax
import jax.numpy as jnp
from jax import lax
from jax.experimental import pallas as pl
from jax.experimental.pallas import tpu as pltpu
from jax.sharding import PartitionSpec as P

CT = 64
SUBBOX_HEADINGS = 128
PT = 128
PP = 256
KIDS = 4
WAVE_NUMBER = 6.0


def waves(count, offset, half):
    doubled = (2 * jnp.arange(count, dtype=jnp.int32) + int(2 * offset))[:, None]
    harmonic = jnp.arange(half + 1, dtype=jnp.int32)[None, :]
    turns = (doubled * harmonic) % (2 * count)
    angle = turns.astype(jnp.float32) * (math.pi / count)
    return jnp.cos(angle), jnp.sin(angle)


def fourier_table(fine_count, coarse_count, offset):
    half = coarse_count // 2
    fine_cos, fine_sin = waves(fine_count, offset, half)
    coarse_cos, coarse_sin = waves(coarse_count, offset, half)
    order = jnp.arange(half + 1)
    weight = jnp.where((order == 0) | (order == half), 1.0, 2.0) / coarse_count
    fine = jnp.concatenate([fine_cos * weight, fine_sin * weight], axis=1)
    coarse = jnp.concatenate([coarse_cos, coarse_sin], axis=1)
    return jnp.dot(fine, coarse.T, precision=lax.Precision.HIGHEST)


def shift_parts(polar_rows):
    polar_angle = math.pi * (polar_rows.astype(jnp.float32) + 0.5) / PT
    heading_radians = 2.0 * math.pi / PP * jnp.arange(PP, dtype=jnp.float32)
    kid_index = jnp.arange(KIDS, dtype=jnp.int32)
    side_x = (2 * (kid_index % 2) - 1).astype(jnp.float32)
    side_y = (2 * (kid_index // 2 % 2) - 1).astype(jnp.float32)
    across = (
        side_x[:, None] * jnp.cos(heading_radians)[None, :]
        + side_y[:, None] * jnp.sin(heading_radians)[None, :]
    )
    phase_arg = WAVE_NUMBER * jnp.sin(polar_angle)[None, :, None] * across[:, None, :]
    return (jnp.cos(phase_arg), jnp.sin(phase_arg))


def lift_sum(widened, cos_part, sin_part):
    real_part = jnp.sum(
        cos_part * widened[..., 0, :, :] - sin_part * widened[..., 1, :, :], axis=-3
    )
    imag_part = jnp.sum(
        cos_part * widened[..., 1, :, :] + sin_part * widened[..., 0, :, :], axis=-3
    )
    return jnp.stack([real_part, imag_part], axis=-3).astype(jnp.bfloat16)


def lower_turn(parents, cos_part, sin_part):
    real_in = jnp.expand_dims(parents[..., 0, :, :].astype(jnp.float32), -3)
    imag_in = jnp.expand_dims(parents[..., 1, :, :].astype(jnp.float32), -3)
    real_out = cos_part * real_in + sin_part * imag_in
    imag_out = cos_part * imag_in - sin_part * real_in
    return jnp.stack([real_out, imag_out], axis=-3).astype(jnp.bfloat16)


def far_kernel(span, list_ref, op_ref, home_ref, field_ref, ops_ref, out_ref, padded):
    rows, slots = list_ref.shape
    empty = ops_ref.shape[0]
    padded[0:empty] = ops_ref[...]
    padded[empty] = jnp.zeros_like(padded[empty])
    thin = out_ref.shape[2]

    def row(r, carry):
        homes, opers = [], []
        for j in range(slots):
            box = list_ref[r, j]
            homes.append(home_ref[jnp.maximum(box, 0)])
            opers.append(jnp.where(box >= 0, op_ref[r, j], empty))
        for start in range(0, thin, span):
            part = pl.ds(start, span)
            real = imag = None
            for j in range(slots):
                a = padded[opers[j], 0, part, :].astype(jnp.float32)
                b = padded[opers[j], 1, part, :].astype(jnp.float32)
                c = field_ref[homes[j], 0, part, :].astype(jnp.float32)
                d = field_ref[homes[j], 1, part, :].astype(jnp.float32)
                re, im = a * c - b * d, a * d + b * c
                real = re if real is None else real + re
                imag = im if imag is None else imag + im
            out_ref[r, 0, part, :] = real.astype(out_ref.dtype)
            out_ref[r, 1, part, :] = imag.astype(out_ref.dtype)
        return carry

    lax.fori_loop(0, rows, row, 0)


def far_sum(field, lists, ops, homes, table, dtype):
    rows, slots = lists.shape
    shape = field.shape[1:]
    span = min(shape[1], 4096 // shape[2])
    smem = pl.BlockSpec(memory_space=pltpu.SMEM)
    vmem = pl.BlockSpec(memory_space=pltpu.VMEM)
    return pl.pallas_call(
        functools.partial(far_kernel, span),
        out_shape=jax.ShapeDtypeStruct((rows,) + shape, dtype),
        in_specs=[smem, smem, smem, vmem, vmem],
        out_specs=vmem,
        scratch_shapes=[pltpu.VMEM((table.shape[0] + 1,) + table.shape[1:], table.dtype)],
        compiler_params=pltpu.CompilerParams(vmem_limit_bytes=32 * 2**20),
        cost_estimate=pl.CostEstimate(
            flops=rows * slots * math.prod(shape) * 4,
            bytes_accessed=field.size * 2 + table.size * 2,
            transcendentals=0,
        ),
    )(lists, ops, homes, field, table)


Z, Y, C = 4, 2, 2
UP, DOWN, SIDE, CORE, PAIR = range(5)
CHUNKS = 4


class Gather:
    def __init__(self, own, slots, rows, send, recv, place):
        self.own, self.slots, self.rows, self.send, self.recv = own, slots, rows, send, recv
        self.z, self.y, self.c = place
        self.started = []

    def slot(self, z, y, c):
        return (z * Y + y) * C + c

    def part(self, slot, h):
        half = self.rows // 2
        return self.slots.at[pl.ds(slot * self.rows + h * half, half)]

    def copy(self, slot, h, way, target, first=False):
        half = self.rows // 2
        source = self.own.at[pl.ds(h * half, half)] if first else self.part(slot, h)
        return pltpu.make_async_remote_copy(
            src_ref=source,
            dst_ref=self.part(slot, h),
            send_sem=self.send.at[way, slot, h],
            recv_sem=self.recv.at[slot, h],
            device_id={"box": target},
            device_id_type=pl.DeviceIdType.MESH,
        )

    def go(self, cond, *args, **kw):
        copy = self.copy(*args, **kw)
        self.started.append((cond, copy))
        pl.when(cond)(lambda: copy.start()) if cond is not None else copy.start()

    def near(self, way):
        z, y, c = self.z, self.y, self.c
        if way == UP:
            return self.slot(jnp.minimum(z + 1, Z - 1), y, c)
        if way == DOWN:
            return self.slot(jnp.maximum(z - 1, 0), y, c)
        if way == SIDE:
            return self.slot(z, 1 - y, c)
        if way == CORE:
            return self.slot(z, y, 1 - c)
        return self.slot(z + 1 - 2 * (z % 2), y, c)

    def arrived(self, cond, slot, h):
        copy = self.copy(slot, h, CORE, self.near(CORE))
        pl.when(cond)(lambda: copy.wait_recv()) if cond is not None else copy.wait_recv()

    def first(self, h):
        mine = self.slot(self.z, self.y, self.c)
        self.go(self.z < Z - 1, mine, h, UP, self.near(UP), first=True)
        self.go(self.z > 0, mine, h, DOWN, self.near(DOWN), first=True)
        self.go(None, mine, h, SIDE, self.near(SIDE), first=True)
        self.go(None, mine, h, CORE, self.near(CORE), first=True)

    def across(self, d):
        for sign in (-1, 1) if d else (1,):
            there = self.z + sign * d
            valid = None if d == 0 else (there >= 0) & (there < Z)
            slot = self.slot(jnp.clip(there, 0, Z - 1), 1 - self.y, self.c)
            for h in range(2):
                self.arrived(valid, slot, h)
                self.go(valid, slot, h, CORE, self.near(CORE))
                if d == 0 and h == 1:
                    self.go(None, slot, h, PAIR, self.near(PAIR))

    def step(self, d):
        for h in range(2):
            for sign in (-1, 1):
                there = self.z + sign * d
                valid = (there >= 0) & (there < Z)
                slot = self.slot(jnp.clip(there, 0, Z - 1), self.y, self.c)
                self.arrived(valid, slot, h)
                onward = valid & ((self.z < Z - 1) if sign < 0 else (self.z > 0))
                self.go(onward, slot, h, UP if sign < 0 else DOWN, self.near(UP if sign < 0 else DOWN))
                side = valid
                if d == 1 and h == 1:
                    side = valid & ((self.z % 2 == 1) if sign < 0 else (self.z % 2 == 0))
                    side = valid & jnp.logical_not(side)
                self.go(side, slot, h, SIDE, self.near(SIDE))
                self.go(valid, slot, h, CORE, self.near(CORE))
        self.across(d - 1)

    def finish(self):
        self.across(Z - 1)
        for z in range(Z):
            for y in range(Y):
                for h in range(2):
                    self.arrived(None, self.slot(z, y, 1 - self.c), h)

    def drain(self):
        for cond, copy in self.started:
            pl.when(cond)(lambda copy=copy: copy.wait_send()) if cond is not None else copy.wait_send()


def translate(lists, op, home, field, padded, r, empty, start, span):
    part = pl.ds(start, span)
    real = imag = None
    for j in range(lists.shape[0]):
        box = lists[j, r]
        at = home[jnp.maximum(box, 0)]
        oper = jnp.where(box >= 0, op[j, r], empty)
        a = padded[oper, 0, part, :].astype(jnp.float32)
        b = padded[oper, 1, part, :].astype(jnp.float32)
        c = field[at, 0, part, :].astype(jnp.float32)
        d = field[at, 1, part, :].astype(jnp.float32)
        re, im = a * c - b * d, a * d + b * c
        real = re if real is None else real + re
        imag = im if imag is None else imag + im
    return real, imag


def whole_kernel(
    child_field, child_list, child_op, child_home, child_ops,
    parent_list, parent_op, parent_home, parent_ops,
    theta_up, phi_up, theta_down, phi_down, cos_ref, sin_ref,
    out_ref,
    child_all, parent_all, polar, child_pad, parent_pad, far, terms,
    c_send, c_recv, p_send, p_recv, x_send, x_recv, f_send, f_recv, here,
):
    box, angle = lax.axis_index("box"), lax.axis_index("angle")
    z, y, c = box // (Y * C), (box // C) % Y, box % C
    children, child_thin = child_field.shape[0], child_field.shape[2]
    parents, parent_thin = parent_list.shape[1], far.shape[3]
    kids_rows, group = children // CHUNKS, parents // CHUNKS
    child_empty, parent_empty = child_ops.shape[0], parent_ops.shape[0]
    MESH = pl.DeviceIdType.MESH
    children_of = Gather(child_field, child_all, children, c_send, c_recv, (z, y, c))
    mine = parent_all.at[pl.ds(box * parents, parents)]
    parents_of = Gather(mine, parent_all, parents, p_send, p_recv, (z, y, c))
    other = {"angle": 1 - angle}

    locals_ = [
        pltpu.make_async_copy(child_field, polar.at[angle], here.at[0]),
        pltpu.make_async_copy(child_field, child_all.at[pl.ds(box * children, children)], here.at[1]),
        pltpu.make_async_copy(child_ops, child_pad.at[pl.ds(0, child_empty)], here.at[2]),
        pltpu.make_async_copy(parent_ops, parent_pad.at[pl.ds(0, parent_empty)], here.at[3]),
    ]
    for copy in locals_:
        copy.start()

    barrier = pltpu.get_barrier_semaphore()
    for way in (SIDE, CORE):
        pl.semaphore_signal(barrier, inc=1, device_id={"box": children_of.near(way)}, device_id_type=MESH)
    pl.semaphore_signal(barrier, inc=1, device_id=other, device_id_type=MESH)

    @pl.when(z < Z - 1)
    def _():
        pl.semaphore_signal(barrier, inc=1, device_id={"box": children_of.near(UP)}, device_id_type=MESH)

    @pl.when(z > 0)
    def _():
        pl.semaphore_signal(barrier, inc=1, device_id={"box": children_of.near(DOWN)}, device_id_type=MESH)

    pl.semaphore_wait(barrier, 5 - (z == 0).astype(jnp.int32) - (z == Z - 1).astype(jnp.int32))

    crossing = []
    for i in range(CHUNKS):
        rows = pl.ds(i * kids_rows, kids_rows)
        crossing.append(
            pltpu.make_async_remote_copy(
                src_ref=child_field.at[rows], dst_ref=polar.at[angle, rows],
                send_sem=x_send.at[i], recv_sem=x_recv.at[i],
                device_id=other, device_id_type=MESH,
            )
        )
        crossing[-1].start()
    for h in range(2):
        children_of.first(h)
    child_pad[child_empty] = jnp.zeros(child_pad.shape[1:], child_pad.dtype)
    parent_pad[parent_empty] = jnp.zeros(parent_pad.shape[1:], parent_pad.dtype)
    for copy in locals_:
        copy.wait()

    up = theta_up[pl.ds(pl.multiple_of(angle * parent_thin, parent_thin), parent_thin), :]
    here_rows = pl.ds(pl.multiple_of(angle * parent_thin, parent_thin), parent_thin)

    def lift(q, carry):
        columns = [
            jnp.concatenate([polar[0, q * KIDS + k, ri], polar[1, q * KIDS + k, ri]], axis=0)
            for k in range(KIDS) for ri in range(2)
        ]
        stretched = jnp.dot(
            up, jnp.concatenate(columns, axis=1), preferred_element_type=jnp.float32
        ).astype(jnp.bfloat16)
        stacked = jnp.concatenate(
            [stretched[:, i * SUBBOX_HEADINGS : (i + 1) * SUBBOX_HEADINGS] for i in range(2 * KIDS)],
            axis=0,
        )
        wide = jnp.dot(stacked, phi_up[...], preferred_element_type=jnp.float32)
        real = imag = 0.0
        for k in range(KIDS):
            co, si = cos_ref[k, here_rows, :], sin_ref[k, here_rows, :]
            wr = wide[2 * k * parent_thin : (2 * k + 1) * parent_thin]
            wi = wide[(2 * k + 1) * parent_thin : (2 * k + 2) * parent_thin]
            real = real + (co * wr - si * wi)
            imag = imag + (co * wi + si * wr)
        parent_all[box * parents + q, 0] = real.astype(jnp.bfloat16)
        parent_all[box * parents + q, 1] = imag.astype(jnp.bfloat16)
        return carry

    for i in range(CHUNKS):
        crossing[i].wait_recv()
        lax.fori_loop(i * group, (i + 1) * group, lift, 0)
        if i % 2:
            parents_of.first(i // 2)

    children_of.step(1)
    parents_of.step(1)
    parents_of.step(2)
    children_of.step(2)
    parents_of.step(3)
    parents_of.finish()

    span = min(parent_thin, 4096 // PP)

    def parent_row(r, carry):
        for start in range(0, parent_thin, span):
            real, imag = translate(
                parent_list, parent_op, parent_home, parent_all, parent_pad, r, parent_empty, start, span
            )
            far[angle, r, 0, pl.ds(start, span), :] = real.astype(jnp.bfloat16)
            far[angle, r, 1, pl.ds(start, span), :] = imag.astype(jnp.bfloat16)
        return carry

    back = []
    for i in range(CHUNKS):
        lax.fori_loop(i * group, (i + 1) * group, parent_row, 0)
        rows = far.at[angle, pl.ds(i * group, group)]
        back.append(
            pltpu.make_async_remote_copy(
                src_ref=rows, dst_ref=rows, send_sem=f_send.at[i], recv_sem=f_recv.at[i],
                device_id=other, device_id_type=MESH,
            )
        )
        back[-1].start()

    down = theta_down[pl.ds(pl.multiple_of(angle * child_thin, child_thin), child_thin), :]

    def lower(q, carry):
        turned = []
        for k in range(KIDS):
            reals, imags = [], []
            for a in range(PT // parent_thin):
                rows = pl.ds(a * parent_thin, parent_thin)
                co, si = cos_ref[k, rows, :], sin_ref[k, rows, :]
                real, imag = far[a, q, 0].astype(jnp.float32), far[a, q, 1].astype(jnp.float32)
                reals.append((co * real + si * imag).astype(jnp.bfloat16))
                imags.append((co * imag - si * real).astype(jnp.bfloat16))
            turned += reals + imags
        narrowed = jnp.dot(
            jnp.concatenate(turned, axis=0), phi_down[...], preferred_element_type=jnp.float32
        ).astype(jnp.bfloat16)
        columns = jnp.concatenate([narrowed[i * PT : (i + 1) * PT] for i in range(2 * KIDS)], axis=1)
        summed = jnp.dot(down, columns, preferred_element_type=jnp.float32).astype(jnp.bfloat16)
        for k in range(KIDS):
            for ri in range(2):
                i = 2 * k + ri
                terms[q * KIDS + k, ri] = summed[:, i * SUBBOX_HEADINGS : (i + 1) * SUBBOX_HEADINGS]
        return carry

    children_of.step(3)
    for i in range(CHUNKS):
        back[i].wait_recv()
        lax.fori_loop(i * group, (i + 1) * group, lower, 0)
    children_of.finish()

    def child_row(r, carry):
        real, imag = translate(
            child_list, child_op, child_home, child_all, child_pad, r, child_empty, 0, child_thin
        )
        out_ref[r, 0] = (real + terms[r, 0].astype(jnp.float32)).astype(jnp.bfloat16)
        out_ref[r, 1] = (imag + terms[r, 1].astype(jnp.float32)).astype(jnp.bfloat16)
        return carry

    lax.fori_loop(0, children, child_row, 0)
    children_of.drain()
    parents_of.drain()
    for copy in crossing + back:
        copy.wait_send()


def whole(fields, tables):
    (
        child_field, child_list, child_op, child_home, child_ops,
        parent_list, parent_op, parent_home, parent_ops,
    ) = fields
    owners, angles = lax.axis_size("box"), lax.axis_size("angle")
    parent_shape = (parent_list.shape[0], 2) + parent_ops.shape[2:]
    smem = pl.BlockSpec(memory_space=pltpu.SMEM)
    vmem = pl.BlockSpec(memory_space=pltpu.VMEM)
    hbm = pl.BlockSpec(memory_space=pl.ANY)
    bf16 = jnp.bfloat16
    dma = pltpu.SemaphoreType.DMA
    return pl.pallas_call(
        whole_kernel,
        out_shape=jax.ShapeDtypeStruct(child_field.shape, bf16),
        in_specs=[hbm, smem, smem, smem, hbm, smem, smem, smem, hbm] + [vmem] * 6,
        out_specs=vmem,
        scratch_shapes=[
            pltpu.VMEM((owners * child_field.shape[0],) + child_field.shape[1:], bf16),
            pltpu.VMEM((owners * parent_shape[0],) + parent_shape[1:], bf16),
            pltpu.VMEM((angles,) + child_field.shape, bf16),
            pltpu.VMEM((child_ops.shape[0] + 1,) + child_ops.shape[1:], bf16),
            pltpu.VMEM((parent_ops.shape[0] + 1,) + parent_ops.shape[1:], bf16),
            pltpu.VMEM((angles,) + parent_shape, bf16),
            pltpu.VMEM(child_field.shape, bf16),
            dma((5, owners, 2)),
            dma((owners, 2)),
            dma((5, owners, 2)),
            dma((owners, 2)),
            dma((CHUNKS,)),
            dma((CHUNKS,)),
            dma((CHUNKS,)),
            dma((CHUNKS,)),
            dma((4,)),
        ],
        compiler_params=pltpu.CompilerParams(
            collective_id=0, has_side_effects=True, vmem_limit_bytes=58 * 2**20
        ),
    )(
        child_field, child_list.T, child_op.T, child_home, child_ops,
        parent_list.T, parent_op.T, parent_home, parent_ops, *tables,
    )


def local(
    child_field,
    child_list,
    child_op,
    child_home,
    child_ops,
    parent_list,
    parent_op,
    parent_home,
    parent_ops,
):
    angle_index = lax.axis_index("angle")
    child_rows = child_field.shape[0]
    parent_rows = parent_list.shape[0]
    child_thin = child_field.shape[2]
    parent_thin = parent_ops.shape[2]
    theta = fourier_table(PT, CT, 0.5)
    phi = fourier_table(PP, SUBBOX_HEADINGS, 0.0)
    theta_up = theta.astype(jnp.bfloat16)
    phi_up = phi.T.astype(jnp.bfloat16)
    theta_down = (theta.T * (CT / PT)).astype(jnp.bfloat16)
    phi_down = (phi * (SUBBOX_HEADINGS / PP)).astype(jnp.bfloat16)
    cos_piece, sin_piece = shift_parts(jnp.arange(PT, dtype=jnp.int32))
    if (lax.axis_size("box"), lax.axis_size("angle")) == (Z * Y * C, 2):
        fields = (
            child_field, child_list, child_op, child_home, child_ops,
            parent_list, parent_op, parent_home, parent_ops,
        )
        return whole(fields, (theta_up, phi_up, theta_down, phi_down, cos_piece, sin_piece))
    whole_polar = lax.all_gather(child_field, "angle", axis=2, tiled=True)
    child_all = lax.all_gather(child_field, "box", axis=0, tiled=True)
    up_rows = lax.dynamic_slice_in_dim(theta_up, angle_index * parent_thin, parent_thin, 0)
    stretched = jnp.einsum(
        "ut,rctp->rcup", up_rows, whole_polar, preferred_element_type=jnp.float32
    ).astype(jnp.bfloat16)
    widened = jnp.einsum("rcup,pv->rcuv", stretched, phi_up, preferred_element_type=jnp.float32)
    local_polar = angle_index * parent_thin + jnp.arange(parent_thin, dtype=jnp.int32)
    cos_local, sin_local = shift_parts(local_polar)
    parent_field = lift_sum(
        widened.reshape(parent_rows, KIDS, 2, parent_thin, PP), cos_local, sin_local
    )
    parent_all = lax.all_gather(parent_field, "box", axis=0, tiled=True)
    child_far = far_sum(child_all, child_list, child_op, child_home, child_ops, jnp.float32)
    parent_far = far_sum(
        parent_all, parent_list, parent_op, parent_home, parent_ops, jnp.bfloat16
    )
    down_rows = lax.dynamic_slice_in_dim(theta_down, angle_index * child_thin, child_thin, 0)
    parents = lax.all_gather(parent_far, "angle", axis=2, tiled=True)
    turned = lower_turn(parents, cos_piece, sin_piece)
    narrowed = jnp.einsum(
        "qkcuv,vp->qkcup", turned, phi_down, preferred_element_type=jnp.float32
    ).astype(jnp.bfloat16)
    summed_term = jnp.einsum(
        "tu,qkcup->qkctp", down_rows, narrowed, preferred_element_type=jnp.float32
    )
    child_term = summed_term.astype(jnp.bfloat16).reshape(
        child_rows, 2, child_thin, SUBBOX_HEADINGS
    )
    child_term = lax.optimization_barrier(child_term)
    return (child_far + child_term.astype(jnp.float32)).astype(jnp.bfloat16)


def solution(mesh):
    return jax.shard_map(
        local,
        mesh=mesh,
        in_specs=(
            P("box", None, "angle", None),
            P("box", None),
            P("box", None),
            P(),
            P(None, None, "angle", None),
            P("box", None),
            P("box", None),
            P(),
            P(None, None, "angle", None),
        ),
        out_specs=P("box", None, "angle", None),
        check_vma=False,
    )
```
